512 devices in a mesh: gx: 32 (over z, x), gy: 16 (over y, core).
Axes of the slice: x: 4, y: 8, z: 8, core: 2. Of those that a mesh axis runs over, the one named last changes fastest.
Arguments:
- prior_basis: float32 [512, 512, 128], P('gx', 'gy'), may hold values from -6 to 6
- cond_x: float32 [512, 512], P('gx', 'gy'), may hold values from 0.5 to 5
- cond_y: float32 [512, 512], P('gx', 'gy'), may hold values from 0.5 to 5
- capacitance: float32 [512, 512], P('gx', 'gy'), may hold values from 0.05 to 1
- pad_mask: int32 [512, 512], P('gx', 'gy'), may hold values 0 or 1
- port_nodes: int32 [128], replicated, may hold values from 0 to 262143
Outputs:
- new_basis: float32 [512, 512, 128], P('gx', 'gy')
- reduced_g: float32 [128, 128], replicated
- reduced_c: float32 [128, 128], replicated
The draws below stay inside these ranges and needn't reach their ends.
Inputs may be any that keep to these rules, and one draw needn't show every extreme that they name: `port_nodes`: a row-major node index into the grid of 512 x 512 nodes.
All inputs are finite; a program needn't handle non-finite values. No bound on the sum of `pad_mask` on one device may be relied on, other than what follows from the above.
Results may differ from the reference program's by a relative error of at most 0.0003.
Values sent between devices are 32-bit elements; how exact they have to be, the bound alone decides.
A program may use at most 64 MiB of HBM per device.

```python
import math
import jax
import jax.numpy as jnp
from jax import lax

P_SIZE = 128
PRIOR = 128
SWEEPS = 4
NX = 512
NY = 512


def with_ends(result, own_key, least, largest):
    longest = result.shape.index(max(result.shape))
    spots = []
    for shift in (0, 1):
        where = [jax.random.randint(jax.random.fold_in(own_key, axis), (), 0, length) for axis, length in enumerate(result.shape)]
        where[longest] = (where[longest] + shift) % result.shape[longest]
        spots.append(tuple(where))
    return result.at[spots[0]].set(least).at[spots[1]].set(largest)


def levels(key, dims, pieces, smallest, top_value):
    factor_of = 1.0
    for axis_at, parts in pieces:
        heights = jax.random.uniform(jax.random.fold_in(jax.random.fold_in(key, 6), axis_at), (parts,), jnp.float32, smallest / len(pieces), top_value / len(pieces))
        factor_of = factor_of * jnp.repeat(jnp.exp(heights), dims[axis_at] // parts).reshape((-1,) + (1,) * (len(dims) - 1 - axis_at))
    return factor_of


def scatter_about(rng, shape, deviation, limit, shards=(), held_as=jnp.bfloat16):
    drawn = deviation * jax.random.normal(rng, shape, jnp.float32)
    if shards:
        drawn = drawn * levels(rng, shape, shards, -0.22, 0.18)
    return jnp.clip(drawn, -limit, limit).astype(held_as)


def setup_inputs(seed: int = 0) -> dict:
    key_of = jax.random.split(jax.random.key(seed), 7)
    prior_basis = scatter_about(key_of[0], (NX, NY, PRIOR), 1.0, 6.0, ((0, 32), (1, 16)), jnp.float32)
    cond_x = jnp.clip(jnp.exp(math.log(5.0) - 2.3025851 * jax.random.uniform(key_of[1], (NX, NY), jnp.float32) ** levels(key_of[1], (NX, NY), ((0, 32), (1, 16)), -0.2, 0.2)), 0.5, 5.0)
    cond_y = jnp.clip(jnp.exp(math.log(5.0) - 2.3025851 * jax.random.uniform(key_of[2], (NX, NY), jnp.float32) ** levels(key_of[2], (NX, NY), ((0, 32), (1, 16)), -0.2, 0.2)), 0.5, 5.0)
    capacitance = jnp.clip(jnp.exp(math.log(1.0) - 2.9957323 * jax.random.uniform(key_of[3], (NX, NY), jnp.float32) ** levels(key_of[3], (NX, NY), ((0, 32), (1, 16)), -0.2, 0.2)), 0.05, 1.0)
    pad_mask = with_ends((jax.random.randint(key_of[4], (NX, NY), 0, 8) < 1).astype(jnp.int32), jax.random.fold_in(key_of[4], 1), 0, 1)
    port_nodes = with_ends(jax.random.randint(key_of[5], (P_SIZE,), 0, NX * NY), jax.random.fold_in(key_of[5], 1), 0, (NX * NY) - 1).astype(jnp.int32)
    return dict(prior_basis=prior_basis, cond_x=cond_x, cond_y=cond_y, capacitance=capacitance, pad_mask=pad_mask, port_nodes=port_nodes)


shift_point = 0.5
supply_conductance = 4.0
port_current = 8.0
highest = lax.Precision.HIGHEST

def coefficients(cond_x, cond_y, capacitance, pad_mask):
    rows = jnp.arange(NX)[:, None]
    cols = jnp.arange(NY)[None, :]
    cx = jnp.where(rows < NX - 1, cond_x, jnp.float32(0.0))
    cy = jnp.where(cols < NY - 1, cond_y, jnp.float32(0.0))
    cx_up = jnp.pad(cx, ((1, 0), (0, 0)))[:-1]
    cy_left = jnp.pad(cy, ((0, 0), (1, 0)))[:, :-1]
    diag_g = cx + cx_up + cy + cy_left + supply_conductance * pad_mask.astype(jnp.float32)
    return (cx, cy, cx_up, cy_left, diag_g)

def near(field, links):
    cx, cy, cx_up, cy_left = links
    ext = jnp.pad(field, ((1, 1), (1, 1), (0, 0)))
    total = cx[:, :, None] * ext[2:, 1:-1] + cx_up[:, :, None] * ext[:-2, 1:-1]
    return total + cy[:, :, None] * ext[1:-1, 2:] + cy_left[:, :, None] * ext[1:-1, :-2]

def inner(left, right, nodes):
    a = left.reshape(-1, left.shape[-1])
    b = right.reshape(-1, right.shape[-1])
    return jnp.einsum('cp,cq->pq', a.astype(jnp.float32), b.astype(jnp.float32), precision=highest, preferred_element_type=jnp.float32) / nodes

def reference(prior_basis, cond_x, cond_y, capacitance, pad_mask, port_nodes):
    cx, cy, cx_up, cy_left, diag_g = coefficients(cond_x, cond_y, capacitance, pad_mask)
    links = (cx, cy, cx_up, cy_left)
    diag = (diag_g + shift_point * capacitance)[:, :, None]
    nodes = NX * NY
    node_ids = jnp.arange(nodes, dtype=jnp.int32).reshape(NX, NY)
    onehot = (node_ids[:, :, None] == port_nodes[None, None, :]).astype(jnp.float32)
    rhs = capacitance[:, :, None] * prior_basis + port_current * onehot
    field = rhs / diag
    for sweep in range(SWEEPS):
        field = (rhs + near(field, links)) / diag
    proj = inner(prior_basis, field, nodes)
    cand = field - jnp.einsum('xyk,kp->xyp', prior_basis, proj, precision=highest)
    gram = inner(cand, cand, nodes)
    lower = jnp.linalg.cholesky(gram)
    flat = cand.reshape(-1, P_SIZE)
    basis_flat = lax.linalg.triangular_solve(lower, flat, left_side=False, lower=True, transpose_a=True)
    new_basis = basis_flat.reshape(NX, NY, P_SIZE)
    g_image = diag_g[:, :, None] * new_basis - near(new_basis, links)
    reduced_g = inner(new_basis, g_image, nodes)
    reduced_c = inner(new_basis, capacitance[:, :, None] * new_basis, nodes)
    return (new_basis, reduced_g, reduced_c)
```

```python
import functools
import math

import jax
import jax.numpy as jnp
from jax import lax
from jax.experimental import pallas as pl
from jax.experimental.pallas import tpu as pltpu
from jax.sharding import PartitionSpec as P

SWEEPS = 4
SHIFT = 0.5
SUPPLY = 4.0
PORT = 8.0
MESH = pl.DeviceIdType.MESH
F32 = jnp.float32
UP, DOWN = SWEEPS, SWEEPS + 1
SIDE = 8
PAD = 8


def mm(a, b, ca, cb):
    return lax.dot_general(
        a, b, (((ca,), (cb,)), ((), ())), precision=lax.Precision.HIGHEST, preferred_element_type=F32
    )


def tn(a, b):
    return mm(a, b, 0, 0)


def nt(a, b):
    return mm(a, b, 1, 1)


def nn(a, b):
    return mm(a, b, 1, 0)


def inverse_factor(matrix):
    n = matrix.shape[0]
    tiles = [matrix[8 * t : 8 * t + 8] for t in range(n // 8)]
    lane = lax.broadcasted_iota(jnp.int32, (8, n), 1)
    sub = lax.broadcasted_iota(jnp.int32, (8, n), 0)

    def row(x, j):
        return jnp.broadcast_to(x[j : j + 1], x.shape)

    def column(x, k):
        return jnp.broadcast_to(x[:, k : k + 1], x.shape)

    rows = []
    for p in range(n // 8):
        g = tiles[p]
        cols = [column(g, 8 * p + j) for j in range(8)]
        kept = jnp.zeros((8, n), F32)
        for j in range(8):
            at = lane == 8 * p + j
            here = sub == j
            rj = row(g, j)
            pivot = row(cols[j], j)
            inv = 1.0 / pivot
            kept = jnp.where(here, jnp.where(at, 1.0, rj) * lax.rsqrt(pivot), kept)
            m = jnp.where(here, -inv, cols[j] * inv)
            for l in range(j + 1, 8):
                cols[l] = jnp.where(here, 0.0, cols[l]) - m * row(cols[l], j)
            g = jnp.where(at, -m, jnp.where(here, 0.0, g) - m * rj)
        rows.append(jnp.where(lane <= sub + 8 * p, kept, 0.0))
        if p + 1 < n // 8:
            w = [row(g, j) for j in range(8)]
            inside = (lane >= 8 * p) & (lane < 8 * p + 8)
            for t in range(p + 1, n // 8):
                x = jnp.where(inside, 0.0, tiles[t])
                for j in range(8):
                    x = x - column(tiles[t], 8 * p + j) * w[j]
                tiles[t] = x
    return rows


def reach(
    ngx, ngy, rows, cols,
    v_hbm, condx_hbm, condy_hbm, cap_hbm, pad_hbm, port_hbm,
    field_out, small_out,
    t0, t1, t2, t3, port, stack, q, qx, vx, cxs, cys, dis, caps, rhs, fa, fb, dgs,
    a0, a1, a2, r10, r11, r12, d0, d1, d2, r20, r21, r22, o0, o1, o2,
    lsem, vsend, vrecv, qsend, qrecv, s1, v1, s2, v2, s3, v3,
):
    gx, gy = lax.axis_index("gx"), lax.axis_index("gy")
    width = 128
    ext = rows + UP + DOWN
    wide = cols + 2 * SIDE
    nx, ny = ngx * rows, ngy * cols
    nodes = nx * ny

    loads = [
        pltpu.make_async_copy(s, d, lsem.at[k])
        for k, (s, d) in enumerate(
            ((condx_hbm, t0), (condy_hbm, t1), (cap_hbm, t2), (pad_hbm, t3), (port_hbm, port),
             (v_hbm, vx.at[pl.ds(UP, rows), pl.ds(SIDE, cols)]))
        )
    ]
    for copy in loads:
        copy.start()

    barrier = pltpu.get_barrier_semaphore()
    around = [(dx, dy) for dx in (-1, 0, 1) for dy in (-1, 0, 1) if dx or dy]

    def beside(dx, dy):
        return lax.rem(gx + ngx + dx, ngx), lax.rem(gy + ngy + dy, ngy)

    for dx, dy in around:
        if dx and dy:
            pl.semaphore_signal(barrier, inc=1, device_id=beside(dx, dy), device_id_type=MESH)

    def others(me, n, f):
        def step(k, c):
            f(lax.rem(me + k, n))
            return c

        lax.fori_loop(1, n, step, 0)

    others(gx, ngx, lambda p: pl.semaphore_signal(barrier, inc=1, device_id=(p, gy), device_id_type=MESH))
    others(gy, ngy, lambda p: pl.semaphore_signal(barrier, inc=1, device_id=(gx, p), device_id_type=MESH))

    stack[...] = jnp.zeros_like(stack)
    for copy in loads[:5]:
        copy.wait()
    for f, ref in enumerate((t0, t1, t2)):
        stack[f * rows : (f + 1) * rows, 0:cols] = ref[...]
    stack[3 * rows : 4 * rows, 0:cols] = t3[...].astype(F32)
    q[...] = stack[...].T[0:cols]
    pl.semaphore_wait(barrier, 4 + ngx - 1 + ngy - 1)

    sent = []
    for k, (dx, dy) in enumerate(around):
        to = beside(dx, dy)
        src_r, dst_r, n_r = ((0, UP + rows, DOWN), (0, UP, rows), (rows - UP, 0, UP))[dx + 1]
        src_c, dst_c, n_c = ((0, SIDE + cols, SIDE), (0, SIDE, cols), (cols - SIDE, 0, SIDE))[dy + 1]
        copy = pltpu.make_async_remote_copy(
            v_hbm.at[pl.ds(src_r, n_r), pl.ds(src_c, n_c)],
            vx.at[pl.ds(dst_r, n_r), pl.ds(dst_c, n_c)],
            vsend.at[k], vrecv.at[k], device_id=to, device_id_type=MESH,
        )
        copy.start()
        sent.append(copy)
        copy = pltpu.make_async_remote_copy(
            q.at[pl.ds(src_c, n_c)],
            qx.at[1 - dx, pl.ds(dst_c, n_c)],
            qsend.at[k], qrecv.at[k], device_id=to, device_id_type=MESH,
        )
        copy.start()
        sent.append(copy)

    def scatter(src, landed, send, recv):
        pc = landed.shape[1]

        def one(p):
            pltpu.make_async_remote_copy(
                src.at[pl.ds(pl.multiple_of(p * pc, 8), pc)], landed.at[gx], send, recv,
                device_id=(p, gy), device_id_type=MESH,
            ).start()

        others(gx, ngx, one)
        landed[gx] = src[pl.ds(pl.multiple_of(gx * pc, 8), pc)]

    def wait(landed, n, sem):
        part = landed.at[pl.ds(0, n - 1)]
        pltpu.make_async_copy(part, part, sem).wait()

    def total(landed):
        x = landed[0]
        for k in range(1, landed.shape[0]):
            x = x + landed[k]
        return x

    def exchange(part, landed, send, recv):
        def one(p):
            pltpu.make_async_remote_copy(
                part, landed.at[gy], send, recv, device_id=(gx, p), device_id_type=MESH
            ).start()

        others(gy, ngy, one)
        landed[gy] = part[...]

    def gather(value, whole, send, recv):
        pc = whole.shape[1]
        whole[gx] = value

        def one(p):
            pltpu.make_async_remote_copy(
                whole.at[gx], whole.at[gx], send, recv, device_id=(p, gy), device_id_type=MESH
            ).start()

        others(gx, ngx, one)

    sets = ((a0, r10, d0, r20, o0), (a1, r11, d1, r21, o1), (a2, r12, d2, r22, o2))

    def first(k):
        scatter(sets[k][0], sets[k][1], s1.at[k], v1.at[k])

    def second(k):
        wait(sets[k][1], ngx, v1.at[k])
        sets[k][2][...] = total(sets[k][1])
        exchange(sets[k][2], sets[k][3], s2.at[k], v2.at[k])

    def third(k):
        wait(sets[k][3], ngy, v2.at[k])
        gather(total(sets[k][3]), sets[k][4], s3.at[k], v3.at[k])

    def last(k):
        wait(sets[k][4], ngx, v3.at[k])

    def block(k, b):
        whole = sets[k][4]
        pc = whole.shape[1]
        per = width // pc if pc <= width else 0
        if per and width % pc == 0:
            return whole[b * per : (b + 1) * per].reshape(width, width)
        return whole[...].reshape(-1, width)[b * width : (b + 1) * width]

    qx[1, SIDE : SIDE + cols] = q[...]
    loads[5].wait()
    own_r, own_c = slice(UP, UP + rows), slice(SIDE, SIDE + cols)
    for i in range(rows):
        k = 2 * rows + i
        caps[UP + i, own_c] = jnp.broadcast_to(q[:, k : k + 1], (cols, width))
    v = vx[own_r, own_c].reshape(rows * cols, width)
    c_own = caps[own_r, own_c].reshape(rows * cols, width)
    a0[0:width] = tn(v, v)
    a0[width : 2 * width] = tn(v, c_own * v)
    first(0)
    for buf in (fa, fb, cys):
        buf[:, 0:PAD] = jnp.zeros((buf.shape[0], PAD, width), F32)
        buf[:, PAD + wide :] = jnp.zeros((buf.shape[0], PAD, width), F32)

    for copy in sent[1::2]:
        copy.wait_recv()
    lane = lax.broadcasted_iota(jnp.int32, (wide, width), 1)
    line = lax.broadcasted_iota(jnp.int32, (wide, width), 0)

    def whole_field(f):
        def at(x, first_row, lane_at):
            return pltpu.roll(x, (lane_at - (f * rows + first_row)) % width, 1)

        above = at(qx[0], rows - UP - 1, 0)
        own = at(qx[1], 0, UP + 1)
        below = at(qx[2], 0, UP + 1 + rows)
        return jnp.where(lane < UP + 1, above, jnp.where(lane < UP + 1 + rows, own, below))

    grow = lax.rem(gx * rows - UP - 1 + lane + nx, nx)
    gcol = lax.rem(gy * cols - SIDE + line + ny, ny)
    cx = jnp.where(grow == nx - 1, 0.0, whole_field(0))
    cy = jnp.where(gcol == ny - 1, 0.0, whole_field(1))
    cp = whole_field(2)
    dg = cx + pltpu.roll(cx, 1, 1) + cy + pltpu.roll(cy, 1, 0) + SUPPLY * whole_field(3)
    di = 1.0 / jnp.where((lane > 0) & (lane <= ext), dg + SHIFT * cp, 1.0)

    def spread(x, i):
        return jnp.broadcast_to(x[:, i + 1 : i + 2], (wide, width))

    cxs[0] = spread(cx, -1)
    for i in range(ext):
        cxs[i + 1] = spread(cx, i)
        cys[i, PAD : PAD + wide] = spread(cy, i)
        dis[i] = spread(di, i)
        caps[i] = spread(cp, i)
    for i in range(rows):
        dgs[i] = jnp.broadcast_to(dg[own_c, UP + i + 1 : UP + i + 2], (cols, width))

    for copy in sent[0::2]:
        copy.wait_recv()
    mid = slice(PAD, PAD + wide)
    rid = lax.rem(gy * cols - SIDE + line + ny, ny)

    def start(i, c):
        node = lax.rem(gx * rows - UP + i + nx, nx) * ny + rid
        r = caps[i] * vx[i] + jnp.where(node == port[...], PORT, 0.0)
        rhs[i] = r
        fa[i, mid] = r * dis[i]
        return c

    lax.fori_loop(0, ext, start, 0)

    src, dst = fa, fb
    for s in range(SWEEPS):
        def sweep(i, c, src=src, dst=dst):
            near = cxs[i + 1] * src[i + 1, mid] + cxs[i] * src[i - 1, mid]
            near = near + cys[i, mid] * src[i, PAD + 1 : PAD + 1 + wide]
            near = near + cys[i, PAD - 1 : PAD - 1 + wide] * src[i, PAD - 1 : PAD - 1 + wide]
            dst[i, mid] = (rhs[i] + near) * dis[i]
            return c

        lax.fori_loop(1 + s, ext - 1 - s, sweep, 0)
        src, dst = dst, src
        if s == 1:
            second(0)

    own_f = slice(PAD + SIDE, PAD + SIDE + cols)
    f = src[own_r, own_f].reshape(rows * cols, width)
    a1[0:width] = tn(v, f)
    a1[width : 2 * width] = tn(f, f)
    first(1)
    third(0)
    field_out[...] = f

    cxo = cxs[UP + 1 : UP + 1 + rows, own_c].reshape(rows * cols, width)
    cyo = cys[own_r, own_f].reshape(rows * cols, width)
    v_below = vx[UP + 1 : UP + 1 + rows, own_c].reshape(rows * cols, width)
    v_right = vx[own_r, SIDE + 1 : SIDE + 1 + cols].reshape(rows * cols, width)
    f_below = src[UP + 1 : UP + 1 + rows, own_f].reshape(rows * cols, width)
    f_right = src[own_r, PAD + SIDE + 1 : PAD + SIDE + 1 + cols].reshape(rows * cols, width)
    dgo = dgs[...].reshape(rows * cols, width)
    uv = cxo * v_below + cyo * v_right
    uf = cxo * f_below + cyo * f_right
    gv = dgo * v - uv
    a2[0:width] = tn(v, gv) - tn(uv, v)
    a2[width : 2 * width] = tn(gv, f) - tn(v, uf)
    a2[2 * width : 3 * width] = tn(f, dgo * f - uf) - tn(uf, f)
    cf = c_own * f
    a2[3 * width : 4 * width] = tn(v, cf)
    a2[4 * width : 5 * width] = tn(f, cf)
    a2[5 * width :] = jnp.zeros((a2.shape[0] - 5 * width, width), F32)
    second(1)
    first(2)
    third(1)
    second(2)
    last(0)
    last(1)

    vv, vcv = block(0, 0) / nodes, block(0, 1) / nodes
    proj, ff = block(1, 0) / nodes, block(1, 1) / nodes
    z = nn(vv, proj) - 2.0 * proj
    gram = ff + tn(proj, z)
    third(2)
    for t, r in enumerate(inverse_factor(gram)):
        small_out[8 * t : 8 * t + 8] = r
    small_out[width : 2 * width] = proj
    last(2)
    vgv, vgf, fgf = (block(2, b) / nodes for b in range(3))
    vcf, fcf = (block(2, b) / nodes for b in range(3, 5))
    small_out[2 * width : 3 * width] = fgf - tn(vgf, proj) + tn(proj, nn(vgv, proj) - vgf)
    small_out[3 * width : 4 * width] = fcf - tn(vcf, proj) + tn(proj, nn(vcv, proj) - vcf)

    for copy in sent:
        copy.wait_send()
    for k in range(3):
        wait(sets[k][1], ngx, s1.at[k])
        wait(sets[k][3], ngy, s2.at[k])
        wait(sets[k][4], ngx, s3.at[k])


def finish(v_ref, f_ref, small_ref, basis_ref, g_ref, c_ref):
    w = 128
    linv = small_ref[0:w]
    y = nt(linv, small_ref[w : 2 * w])
    basis_ref[...] = nt(f_ref[...], linv) - nt(v_ref[...], y)
    g_ref[...] = nt(nn(linv, small_ref[2 * w : 3 * w]), linv)
    c_ref[...] = nt(nn(linv, small_ref[3 * w : 4 * w]), linv)


def per_device(prior_basis, cond_x, cond_y, capacitance, pad_mask, port_nodes):
    rows, cols, width = prior_basis.shape
    ngx, ngy = lax.axis_size("gx"), lax.axis_size("gy")
    ext, wide = rows + UP + DOWN, cols + 2 * SIDE
    hbm = pl.BlockSpec(memory_space=pltpu.HBM)
    vmem = pl.BlockSpec(memory_space=pltpu.VMEM)

    def buf(*shape):
        return pltpu.VMEM(shape, F32)

    dma = pltpu.SemaphoreType.DMA
    pcs = (2 * width // ngx, 2 * width // ngx, 6 * width // ngx)
    scratch = [buf(rows, cols)] * 3 + [pltpu.VMEM((rows, cols), jnp.int32), pltpu.VMEM((1, width), jnp.int32)]
    scratch += [buf(width, width), buf(cols, width), buf(3, wide, width), buf(ext, wide, width)]
    scratch += [buf(ext + 1, wide, width), buf(ext, wide + 2 * PAD, width), buf(ext, wide, width)]
    scratch += [buf(ext, wide, width), buf(ext, wide, width)]
    scratch += [buf(ext, wide + 2 * PAD, width), buf(ext, wide + 2 * PAD, width), buf(rows, cols, width)]
    scratch += [buf(pc * ngx, width) for pc in pcs]
    scratch += [buf(ngx, pc, width) for pc in pcs]
    scratch += [buf(pc, width) for pc in pcs]
    scratch += [buf(ngy, pc, width) for pc in pcs]
    scratch += [buf(ngx, pc, width) for pc in pcs]
    scratch += [dma((6,)), dma((8,)), dma((8,)), dma((8,)), dma((8,))] + [dma((3,))] * 6
    field, small = pl.pallas_call(
        functools.partial(reach, ngx, ngy, rows, cols),
        out_shape=(
            jax.ShapeDtypeStruct((rows * cols, width), F32),
            jax.ShapeDtypeStruct((4 * width, width), F32),
        ),
        in_specs=[hbm] * 6,
        out_specs=(vmem, vmem),
        scratch_shapes=scratch,
        compiler_params=pltpu.CompilerParams(
            collective_id=0, has_side_effects=True, vmem_limit_bytes=40 * 1024 * 1024
        ),
    )(prior_basis, cond_x, cond_y, capacitance, pad_mask, port_nodes.reshape(1, width))
    basis, g, c = pl.pallas_call(
        finish,
        out_shape=(
            jax.ShapeDtypeStruct((rows * cols, width), F32),
            jax.ShapeDtypeStruct((width, width), F32),
            jax.ShapeDtypeStruct((width, width), F32),
        ),
        in_specs=[vmem] * 3,
        out_specs=(vmem,) * 3,
        compiler_params=pltpu.CompilerParams(vmem_limit_bytes=16 * 1024 * 1024),
    )(prior_basis.reshape(rows * cols, width), field, small)
    return basis.reshape(rows, cols, width), g, c


def solution(mesh):
    tile = P("gx", "gy")
    return jax.shard_map(
        per_device,
        mesh=mesh,
        in_specs=(P("gx", "gy", None), tile, tile, tile, tile, P()),
        out_specs=(P("gx", "gy", None), P(), P()),
        check_vma=False,
    )
```

```python
import functools
import math

import jax
import jax.numpy as jnp
from jax import lax
from jax.experimental import pallas as pl
from jax.experimental.pallas import tpu as pltpu
from jax.sharding import PartitionSpec as P

SWEEPS = 4
SHIFT = 0.5
SUPPLY = 4.0
PORT = 8.0
MESH = pl.DeviceIdType.MESH
F32 = jnp.float32
UP, DOWN = SWEEPS, SWEEPS + 1
SIDE = 8
PAD = 8


def mm(a, b, ca, cb):
    return lax.dot_general(
        a, b, (((ca,), (cb,)), ((), ())), precision=lax.Precision.HIGHEST, preferred_element_type=F32
    )


def tn(a, b):
    return mm(a, b, 0, 0)


def nt(a, b):
    return mm(a, b, 1, 1)


def nn(a, b):
    return mm(a, b, 1, 0)


def inverse_factor(matrix):
    n = matrix.shape[0]
    tiles = [matrix[8 * t : 8 * t + 8] for t in range(n // 8)]
    lane = lax.broadcasted_iota(jnp.int32, (8, n), 1)
    sub = lax.broadcasted_iota(jnp.int32, (8, n), 0)

    def row(x, j):
        return jnp.broadcast_to(x[j : j + 1], x.shape)

    def column(x, k):
        return jnp.broadcast_to(x[:, k : k + 1], x.shape)

    for p in range(n // 8):
        g = tiles[p]
        cols = [column(g, 8 * p + j) for j in range(8)]
        kept = jnp.zeros((8, n), F32)
        for j in range(8):
            at = lane == 8 * p + j
            here = sub == j
            rj = row(g, j)
            pivot = row(cols[j], j)
            inv = 1.0 / pivot
            kept = jnp.where(here, jnp.where(at, 1.0, rj) * lax.rsqrt(pivot), kept)
            m = jnp.where(here, -inv, cols[j] * inv)
            for l in range(j + 1, 8):
                cols[l] = jnp.where(here, 0.0, cols[l]) - m * row(cols[l], j)
            g = jnp.where(at, -m, jnp.where(here, 0.0, g) - m * rj)
        yield jnp.where(lane <= sub + 8 * p, kept, 0.0)
        if p + 1 < n // 8:
            w = [row(g, j) for j in range(8)]
            inside = (lane >= 8 * p) & (lane < 8 * p + 8)
            for t in range(p + 1, n // 8):
                x = jnp.where(inside, 0.0, tiles[t])
                for j in range(8):
                    x = x - column(tiles[t], 8 * p + j) * w[j]
                tiles[t] = x


def reach(
    ngx, ngy, rows, cols,
    v_hbm, condx_hbm, condy_hbm, cap_hbm, pad_hbm, port_hbm,
    field_out, small_out,
    t0, t1, t2, t3, port, stack, q, qx, vx, cxs, cys, dis, caps, rhs, fa, fb, dgs,
    a0, a1, a2, r10, r11, r12, d0, d1, d2, r20, r21, r22, o0, o1,
    rc2, h2, hw2, lsem, csend, crecv, vsend, vrecv, qsend, qrecv, s1, v1, s2, v2, s3, v3,
):
    gx, gy = lax.axis_index("gx"), lax.axis_index("gy")
    width = 128
    ext = rows + UP + DOWN
    wide = cols + 2 * SIDE
    nx, ny = ngx * rows, ngy * cols
    nodes = nx * ny

    barrier = pltpu.get_barrier_semaphore()
    around = [(dx, dy) for dx in (-1, 0, 1) for dy in (-1, 0, 1) if dx or dy]

    def beside(dx, dy):
        return lax.rem(gx + ngx + dx, ngx), lax.rem(gy + ngy + dy, ngy)

    for dx, dy in around:
        pl.semaphore_signal(barrier, inc=1, device_id=beside(dx, dy), device_id_type=MESH)

    def others(me, n, f, lo=1):
        def step(k, c):
            f(lax.rem(me + k, n))
            return c

        lax.fori_loop(lo, n + 1 - lo, step, 0)

    others(gx, ngx, lambda p: pl.semaphore_signal(barrier, inc=1, device_id=(p, gy), device_id_type=MESH), 2)
    others(gy, ngy, lambda p: pl.semaphore_signal(barrier, inc=1, device_id=(gx, p), device_id_type=MESH), 2)

    loads = [
        pltpu.make_async_copy(s, d, lsem.at[k])
        for k, (s, d) in enumerate(
            ((condx_hbm, t0), (condy_hbm, t1), (cap_hbm, t2), (pad_hbm, t3), (port_hbm, port),
             (v_hbm, vx.at[pl.ds(UP, rows), pl.ds(SIDE, cols)]))
        )
    ]
    for copy in loads:
        copy.start()

    stack[...] = jnp.zeros_like(stack)
    for copy in loads[:5]:
        copy.wait()
    for f, ref in enumerate((t0, t1, t2)):
        stack[f * rows : (f + 1) * rows, 0:cols] = ref[...]
    stack[3 * rows : 4 * rows, 0:cols] = t3[...].astype(F32)
    q[...] = stack[...].T[0:cols]
    pl.semaphore_wait(barrier, 4 + ngx - 1 + ngy - 1)

    sent = []
    for k, (dx, dy) in enumerate(around):
        to = beside(dx, dy)
        src_r, dst_r, n_r = ((0, UP + rows, DOWN), (0, UP, rows), (rows - UP, 0, UP))[dx + 1]
        src_c, dst_c, n_c = ((0, SIDE + cols, SIDE), (0, SIDE, cols), (cols - SIDE, 0, SIDE))[dy + 1]
        copy = pltpu.make_async_remote_copy(
            v_hbm.at[pl.ds(src_r, n_r), pl.ds(src_c, n_c)],
            vx.at[pl.ds(dst_r, n_r), pl.ds(dst_c, n_c)],
            vsend.at[k], vrecv.at[k], device_id=to, device_id_type=MESH,
        )
        copy.start()
        sent.append(copy)
        copy = pltpu.make_async_remote_copy(
            q.at[pl.ds(src_c, n_c)],
            qx.at[1 - dx, pl.ds(dst_c, n_c)],
            qsend.at[k], qrecv.at[k], device_id=to, device_id_type=MESH,
        )
        copy.start()
        sent.append(copy)

    def scatter(src, landed, send, recv):
        pc = landed.shape[1]

        def one(p):
            pltpu.make_async_remote_copy(
                src.at[pl.ds(pl.multiple_of(p * pc, 8), pc)], landed.at[gx], send, recv,
                device_id=(p, gy), device_id_type=MESH,
            ).start()

        others(gx, ngx, one)
        landed[gx] = src[pl.ds(pl.multiple_of(gx * pc, 8), pc)]

    def wait(landed, n, sem):
        part = landed.at[pl.ds(0, n - 1)]
        pltpu.make_async_copy(part, part, sem).wait()

    def total(landed):
        x = landed[0]
        for k in range(1, landed.shape[0]):
            x = x + landed[k]
        return x

    def exchange(part, landed, send, recv):
        slots = landed.shape[0]
        step = ngy // slots
        me = gy // step

        def one(p):
            pltpu.make_async_remote_copy(
                part, landed.at[me], send, recv,
                device_id=(gx, p * step + lax.rem(gy, step)), device_id_type=MESH,
            ).start()

        others(me, slots, one)
        landed[me] = part[...]

    def gather(value, whole, send, recv):
        whole[gx] = value

        def one(p):
            pltpu.make_async_remote_copy(
                whole.at[gx], whole.at[gx], send, recv, device_id=(p, gy), device_id_type=MESH
            ).start()

        others(gx, ngx, one)

    core = lax.rem(gy, 2)
    mate = (gx, gy + 1 - 2 * core)
    half = 2 * width
    to_mate = pltpu.make_async_remote_copy(
        a2.at[pl.ds(pl.multiple_of((1 - core) * half, 8), half)], rc2, csend.at[0], crecv.at[0],
        device_id=mate, device_id_type=MESH,
    )
    back = pltpu.make_async_remote_copy(
        hw2.at[core], hw2.at[core], csend.at[1], crecv.at[1], device_id=mate, device_id_type=MESH
    )

    sets = ((a0, r10, d0, r20, o0), (a1, r11, d1, r21, o1), (h2, r12, d2, r22, hw2.at[core]))

    def first(k):
        scatter(sets[k][0], sets[k][1], s1.at[k], v1.at[k])

    def second(k):
        wait(sets[k][1], ngx, v1.at[k])
        sets[k][2][...] = total(sets[k][1])
        exchange(sets[k][2], sets[k][3], s2.at[k], v2.at[k])

    def third(k):
        wait(sets[k][3], sets[k][3].shape[0], v2.at[k])
        gather(total(sets[k][3]), sets[k][4], s3.at[k], v3.at[k])

    def last(k):
        wait(sets[k][4], ngx, v3.at[k])

    def block(k, b):
        return sets[k][4][...].reshape(2 * width, width)[b * width : (b + 1) * width]

    wr = lax.broadcasted_iota(jnp.int32, (width, width), 0)
    wc = lax.broadcasted_iota(jnp.int32, (width, width), 1)

    qx[1, SIDE : SIDE + cols] = q[...]
    loads[5].wait()
    own_r, own_c = slice(UP, UP + rows), slice(SIDE, SIDE + cols)
    for i in range(rows):
        k = 2 * rows + i
        caps[UP + i, own_c] = jnp.broadcast_to(q[:, k : k + 1], (cols, width))
    v = vx[own_r, own_c].reshape(rows * cols, width)
    c_own = caps[own_r, own_c].reshape(rows * cols, width)
    a0[0:width] = tn(v, v)
    a0[width : 2 * width] = tn(v, c_own * v)
    first(0)
    for buf in (fa, fb, cys):
        buf[:, 0:PAD] = jnp.zeros((buf.shape[0], PAD, width), F32)
        buf[:, PAD + wide :] = jnp.zeros((buf.shape[0], PAD, width), F32)

    for copy in sent[1::2]:
        copy.wait_recv()
    lane = lax.broadcasted_iota(jnp.int32, (wide, width), 1)
    line = lax.broadcasted_iota(jnp.int32, (wide, width), 0)

    def whole_field(f):
        def at(x, first_row, lane_at):
            return pltpu.roll(x, (lane_at - (f * rows + first_row)) % width, 1)

        above = at(qx[0], rows - UP - 1, 0)
        own = at(qx[1], 0, UP + 1)
        below = at(qx[2], 0, UP + 1 + rows)
        return jnp.where(lane < UP + 1, above, jnp.where(lane < UP + 1 + rows, own, below))

    grow = lax.rem(gx * rows - UP - 1 + lane + nx, nx)
    gcol = lax.rem(gy * cols - SIDE + line + ny, ny)
    cx = jnp.where(grow == nx - 1, 0.0, whole_field(0))
    cy = jnp.where(gcol == ny - 1, 0.0, whole_field(1))
    cp = whole_field(2)
    dg = cx + pltpu.roll(cx, 1, 1) + cy + pltpu.roll(cy, 1, 0) + SUPPLY * whole_field(3)
    di = 1.0 / jnp.where((lane > 0) & (lane <= ext), dg + SHIFT * cp, 1.0)

    def spread(x, i):
        return jnp.broadcast_to(x[:, i + 1 : i + 2], (wide, width))

    cxs[0] = spread(cx, -1)
    for i in range(ext):
        cxs[i + 1] = spread(cx, i)
        cys[i, PAD : PAD + wide] = spread(cy, i)
        dis[i] = spread(di, i)
        caps[i] = spread(cp, i)
    for i in range(rows):
        dgs[i] = jnp.broadcast_to(dg[own_c, UP + i + 1 : UP + i + 2], (cols, width))

    for copy in sent[0::2]:
        copy.wait_recv()
    mid = slice(PAD, PAD + wide)
    rid = lax.rem(gy * cols - SIDE + line + ny, ny)

    def start(i, c):
        node = lax.rem(gx * rows - UP + i + nx, nx) * ny + rid
        r = caps[i] * vx[i] + jnp.where(node == port[...], PORT, 0.0)
        rhs[i] = r
        fa[i, mid] = r * dis[i]
        return c

    lax.fori_loop(0, ext, start, 0)

    src, dst = fa, fb
    for s in range(SWEEPS):
        def sweep(i, c, src=src, dst=dst):
            near = cxs[i + 1] * src[i + 1, mid] + cxs[i] * src[i - 1, mid]
            near = near + cys[i, mid] * src[i, PAD + 1 : PAD + 1 + wide]
            near = near + cys[i, PAD - 1 : PAD - 1 + wide] * src[i, PAD - 1 : PAD - 1 + wide]
            dst[i, mid] = (rhs[i] + near) * dis[i]
            return c

        lax.fori_loop(1 + s, ext - 1 - s, sweep, 0)
        src, dst = dst, src

    own_f = slice(PAD + SIDE, PAD + SIDE + cols)
    f = src[own_r, own_f].reshape(rows * cols, width)
    a1[0:width] = tn(v, f)
    a1[width : 2 * width] = tn(f, f)
    first(1)
    field_out[...] = f

    cxo = cxs[UP + 1 : UP + 1 + rows, own_c].reshape(rows * cols, width)
    cyo = cys[own_r, own_f].reshape(rows * cols, width)
    v_below = vx[UP + 1 : UP + 1 + rows, own_c].reshape(rows * cols, width)
    v_right = vx[own_r, SIDE + 1 : SIDE + 1 + cols].reshape(rows * cols, width)
    f_below = src[UP + 1 : UP + 1 + rows, own_f].reshape(rows * cols, width)
    f_right = src[own_r, PAD + SIDE + 1 : PAD + SIDE + 1 + cols].reshape(rows * cols, width)
    dgo = dgs[...].reshape(rows * cols, width)
    uv = cxo * v_below + cyo * v_right
    uf = cxo * f_below + cyo * f_right
    gv = dgo * v - uv
    vgv = tn(v, gv) - tn(uv, v)
    fgf = tn(f, dgo * f - uf) - tn(uf, f)
    cf = c_own * f
    fcf = tn(f, cf)
    corner = jnp.sum(jnp.where(wr == wc, fcf, 0.0), axis=0, keepdims=True)
    spare = jnp.where(wr == 0, corner, jnp.where(wc == width - 1, pltpu.roll(corner, width - 1, 1), 0.0))
    a2[0:width] = jnp.where(wr >= wc, vgv, spare)
    a2[width : 2 * width] = jnp.where(wr >= wc, fgf, fcf)
    a2[2 * width : 3 * width] = tn(gv, f) - tn(v, uf)
    a2[3 * width : 4 * width] = tn(v, cf)
    to_mate.start()
    second(0)
    to_mate.wait_recv()
    h2[...] = a2[pl.ds(pl.multiple_of(core * half, 8), half)] + rc2[...]
    first(2)
    second(1)
    third(0)
    second(2)
    third(1)
    last(0)
    third(2)
    last(1)
    vv, vcv = block(0, 0) / nodes, block(0, 1) / nodes
    proj, ff = block(1, 0) / nodes, block(1, 1) / nodes
    z = nn(vv, proj) - 2.0 * proj
    gram = ff + tn(proj, z)
    for t, r in enumerate(inverse_factor(gram)):
        small_out[8 * t : 8 * t + 8] = r
        if t == 10:
            last(2)
            back.start()
    small_out[width : 2 * width] = proj
    back.wait_recv()
    sums = hw2[...].reshape(4, width, width) / nodes

    def both(tri, keep):
        return jnp.where(keep, tri, 0.0) + jnp.where(wr == wc, 0.0, jnp.where(keep, tri, 0.0)).T

    vgf, vcf = sums[2], sums[3]
    vgv, fgf = both(sums[0], wr >= wc), both(sums[1], wr >= wc)
    corner = jnp.where(wc[0:1] == 0, pltpu.roll(sums[0, 1:2], 1, 1), sums[0, 0:1])
    fcf = both(sums[1], wr < wc) + jnp.where(wr == wc, corner, 0.0)
    small_out[2 * width : 3 * width] = fgf - tn(vgf, proj) + tn(proj, nn(vgv, proj) - vgf)
    small_out[3 * width : 4 * width] = fcf - tn(vcf, proj) + tn(proj, nn(vcv, proj) - vcf)

    for copy in sent + [to_mate, back]:
        copy.wait_send()
    for k in range(3):
        wait(sets[k][1], ngx, s1.at[k])
        wait(sets[k][3], sets[k][3].shape[0], s2.at[k])
        wait(sets[k][4], ngx, s3.at[k])


def finish(v_ref, f_ref, small_ref, basis_ref, g_ref, c_ref):
    w = 128
    linv = small_ref[0:w]
    y = nt(linv, small_ref[w : 2 * w])
    basis_ref[...] = nt(f_ref[...], linv) - nt(v_ref[...], y)
    g_ref[...] = nt(nn(linv, small_ref[2 * w : 3 * w]), linv)
    c_ref[...] = nt(nn(linv, small_ref[3 * w : 4 * w]), linv)


def per_device(prior_basis, cond_x, cond_y, capacitance, pad_mask, port_nodes):
    rows, cols, width = prior_basis.shape
    ngx, ngy = lax.axis_size("gx"), lax.axis_size("gy")
    ext, wide = rows + UP + DOWN, cols + 2 * SIDE
    hbm = pl.BlockSpec(memory_space=pltpu.HBM)
    vmem = pl.BlockSpec(memory_space=pltpu.VMEM)

    def buf(*shape):
        return pltpu.VMEM(shape, F32)

    dma = pltpu.SemaphoreType.DMA
    pc = 2 * width // ngx
    scratch = [buf(rows, cols)] * 3 + [pltpu.VMEM((rows, cols), jnp.int32), pltpu.VMEM((1, width), jnp.int32)]
    scratch += [buf(width, width), buf(cols, width), buf(3, wide, width), buf(ext, wide, width)]
    scratch += [buf(ext + 1, wide, width), buf(ext, wide + 2 * PAD, width), buf(ext, wide, width)]
    scratch += [buf(ext, wide, width), buf(ext, wide, width)]
    scratch += [buf(ext, wide + 2 * PAD, width), buf(ext, wide + 2 * PAD, width), buf(rows, cols, width)]
    scratch += [buf(2 * width, width), buf(2 * width, width), buf(4 * width, width)]
    scratch += [buf(ngx, pc, width)] * 3 + [buf(pc, width)] * 3
    scratch += [buf(ngy, pc, width), buf(ngy, pc, width), buf(ngy // 2, pc, width)]
    scratch += [buf(ngx, pc, width)] * 2
    scratch += [buf(2 * width, width), buf(2 * width, width), buf(2, ngx, 2 * width // ngx, width)]
    scratch += [dma((6,)), dma((2,)), dma((2,)), dma((8,)), dma((8,)), dma((8,)), dma((8,))] + [dma((3,))] * 6
    field, small = pl.pallas_call(
        functools.partial(reach, ngx, ngy, rows, cols),
        out_shape=(
            jax.ShapeDtypeStruct((rows * cols, width), F32),
            jax.ShapeDtypeStruct((4 * width, width), F32),
        ),
        in_specs=[hbm] * 6,
        out_specs=(vmem, vmem),
        scratch_shapes=scratch,
        compiler_params=pltpu.CompilerParams(
            collective_id=0, has_side_effects=True, vmem_limit_bytes=60 * 1024 * 1024
        ),
    )(prior_basis, cond_x, cond_y, capacitance, pad_mask, port_nodes.reshape(1, width))
    basis, g, c = pl.pallas_call(
        finish,
        out_shape=(
            jax.ShapeDtypeStruct((rows * cols, width), F32),
            jax.ShapeDtypeStruct((width, width), F32),
            jax.ShapeDtypeStruct((width, width), F32),
        ),
        in_specs=[vmem] * 3,
        out_specs=(vmem,) * 3,
        compiler_params=pltpu.CompilerParams(vmem_limit_bytes=60 * 1024 * 1024),
    )(prior_basis.reshape(rows * cols, width), field, small)
    return basis.reshape(rows, cols, width), g, c


def solution(mesh):
    tile = P("gx", "gy")
    return jax.shard_map(
        per_device,
        mesh=mesh,
        in_specs=(P("gx", "gy", None), tile, tile, tile, tile, P()),
        out_specs=(P("gx", "gy", None), P(), P()),
        check_vma=False,
    )
```
